32 devices in a mesh: group: 2 (over y), shard: 16 (over z, x, core).
Axes of the slice: x: 2, y: 2, z: 4, core: 2. Of those that a mesh axis runs over, the one named last changes fastest.
Arguments:
- features: bfloat16 [32768, 768], P('shard'), may hold values from -6 to 6
- seed_rows: int32 [8192], P(('group', 'shard')), parts along dimension 0, may hold values from 0 to 2047
- request_rows: int32 [32, 16, 2, 8], P(('group', 'shard')), parts along dimension 0, may hold values from 0 to 2047
- block_counts: int32 [32, 16], P(('group', 'shard')), parts along dimension 0, may hold values from 0 to 2, as said below
- tiles: bfloat16 [32, 32, 8, 128], P(('group', 'shard')), parts along dimension 0, may hold values from -0.5 to 0.5
- tile_seed_block: int32 [32, 32], P(('group', 'shard')), parts along dimension 0, may hold values from 0 to 1
- w_self: bfloat16 [768, 1024], replicated, may hold values from -0.21875 to 0.21875
- w_neigh: bfloat16 [768, 1024], replicated, may hold values from -0.21875 to 0.21875
- grad_out: bfloat16 [8192, 1024], P(('group', 'shard')), parts along dimension 0, may hold values from -0.09375 to 0.09375
Outputs:
- hidden: bfloat16 [8192, 1024], P(('group', 'shard')), parts along dimension 0
- grad_self: float32 [1536, 1024], P(('group', 'shard')), parts along dimension 0
- grad_neigh: float32 [1536, 1024], P(('group', 'shard')), parts along dimension 0
The draws below stay inside these ranges and needn't reach their ends.
There are 2 independent parts, one for each index of `group`. The reference program is written for one: setup_inputs(seed, part) draws one part's arguments, and reference() takes and returns one part's arrays. A program takes and returns all parts, laid end to end along the dimension named above; an argument that names none is the same for every part. Nothing has to cross between parts.
Inputs may be any that keep to these rules, and one draw needn't show every extreme that they name: Trainer t pulls block_counts[t, o] blocks from owner o; request_rows beyond that count are padding and are not used. In every draw some owner gets 2 blocks from every trainer. `seed_rows`: row numbers within the trainer's own rows. `tile_seed_block`: seed block of a slot's tile.
All inputs are finite; a program needn't handle non-finite values.
Results may differ from the reference program's by a relative error of at most 0.0053.
Values may be sent and summed in bfloat16 or wider, within the bound.
A program may use at most 64 MiB of HBM per device.

```python
import jax
import jax.numpy as jnp
from jax import lax

INPUT_WIDTH = 768
H = 1024
ROWS_DEV = 2048
TRAINER_SEEDS = 256
SEED_BLOCK_SIZE = 128
BLOCK_NODE_ROWS = 8
CAP = 2
TRAINER_SLOTS = 32
NODES = 32768
TOTAL_SEEDS = 4096
N_SHARD = 16


def draw_block_counts(key, part):
    key = jax.random.fold_in(key, 11)
    first_key, second_key, third_key = jax.random.split(key, 3)
    popular = jax.random.randint(first_key, (N_SHARD,), 0, 4) == 0
    chosen = jax.random.randint(second_key, (), 0, N_SHARD)
    popular = popular | (jnp.arange(N_SHARD) == chosen)
    baseline = jax.random.randint(third_key, (N_SHARD, N_SHARD), 0, CAP + 1)
    return jnp.where(popular[None, :], CAP, baseline).astype(jnp.int32)


def touch_ends(entries, stream_key, low, top_value):
    longest = entries.shape.index(max(entries.shape))
    spots = []
    for shift in (0, 1):
        where = [jax.random.randint(jax.random.fold_in(stream_key, axis), (), 0, length) for axis, length in enumerate(entries.shape)]
        where[longest] = (where[longest] + shift) % entries.shape[longest]
        spots.append(tuple(where))
    return entries.at[spots[0]].set(low).at[spots[1]].set(top_value)


def levels(stream_key, extent, cuts, smallest, largest):
    def one(axis_at, shards_of):
        heights = jax.random.uniform(jax.random.fold_in(jax.random.fold_in(stream_key, 6), axis_at), (shards_of,), jnp.float32, smallest / len(cuts), largest / len(cuts))
        return jnp.repeat(jnp.exp(heights), extent[axis_at] // shards_of).reshape((-1,) + (1,) * (len(extent) - axis_at - 1))

    level = one(*cuts[0])
    for cut in cuts[1:]:
        level = level * one(*cut)
    return level


def noise(rng, shape, width, bound, cuts=(), kind=jnp.bfloat16):
    level = levels(rng, shape, cuts, -0.22, 0.18) if cuts else 1.0
    array = jax.random.normal(rng, shape, jnp.float32) * width * level
    return jnp.minimum(jnp.maximum(array, -bound), bound).astype(kind)


def setup_inputs(seed: int = 0, part: int = 0) -> dict:
    splits = jax.random.split(jax.random.key(seed), 10)
    part_keys = jax.random.split(jax.random.fold_in(splits[9], part), 10)
    features = noise(splits[0], (NODES, INPUT_WIDTH), 1.0, 6.0, ((0, 16),))
    seed_rows = touch_ends(jax.random.randint(part_keys[1], (TOTAL_SEEDS,), 0, ROWS_DEV), jax.random.fold_in(part_keys[1], 1), 0, ROWS_DEV - 1).astype(jnp.int32)
    request_rows = touch_ends(jax.random.randint(part_keys[2], (N_SHARD, N_SHARD, CAP, BLOCK_NODE_ROWS), 0, ROWS_DEV), jax.random.fold_in(part_keys[2], 1), 0, ROWS_DEV - 1).astype(jnp.int32)
    block_counts = draw_block_counts(jax.random.fold_in(jax.random.fold_in(splits[9], part), 71), part)
    tiles = noise(part_keys[4], (N_SHARD, TRAINER_SLOTS, BLOCK_NODE_ROWS, SEED_BLOCK_SIZE), (TRAINER_SLOTS * BLOCK_NODE_ROWS // 2) ** -0.5, 0.5, ((0, 16),))
    tile_seed_block = touch_ends(jax.random.randint(part_keys[5], (N_SHARD, TRAINER_SLOTS), 0, TRAINER_SEEDS // SEED_BLOCK_SIZE), jax.random.fold_in(part_keys[5], 1), 0, (TRAINER_SEEDS // SEED_BLOCK_SIZE) - 1).astype(jnp.int32)
    w_self = noise(splits[6], (INPUT_WIDTH, H), INPUT_WIDTH ** -0.5, 0.21875)
    w_neigh = noise(splits[7], (INPUT_WIDTH, H), INPUT_WIDTH ** -0.5, 0.21875)
    grad_out = noise(part_keys[8], (TOTAL_SEEDS, H), TOTAL_SEEDS ** -0.5, 0.09375, ((0, 16),))
    return {"features": features, "seed_rows": seed_rows, "request_rows": request_rows, "block_counts": block_counts, "tiles": tiles, "tile_seed_block": tile_seed_block, "w_self": w_self, "w_neigh": w_neigh, "grad_out": grad_out}


def activate(values):
    return jax.nn.gelu(values, approximate=True)

def reference(features, seed_rows, request_rows, block_counts, tiles, tile_seed_block, w_self, w_neigh, grad_out):
    shards = N_SHARD
    table = features.reshape(shards, ROWS_DEV, INPUT_WIDTH)
    seed_view = seed_rows.reshape(shards, TRAINER_SEEDS)
    grad_view = grad_out.reshape(shards, TRAINER_SEEDS, H)
    blocks = TRAINER_SEEDS // SEED_BLOCK_SIZE
    owners = jnp.arange(shards, dtype=jnp.int32)

    def per_trainer(carry, inputs):
        total_self, total_neigh = carry
        trainer, seed_local, requests, counts, tile_collection, tile_owner, grad_local = inputs
        selected_blocks = table[owners[:, None, None], requests]
        usable_mask = jnp.arange(CAP, dtype=jnp.int32)[None, :] < counts[:, None]
        neighbour_frontier = jnp.where(usable_mask[:, :, None, None], selected_blocks, jnp.zeros((), features.dtype)).reshape(TRAINER_SLOTS * BLOCK_NODE_ROWS, INPUT_WIDTH)
        messages = jnp.dot(neighbour_frontier, w_neigh, preferred_element_type=jnp.float32).astype(jnp.bfloat16)
        select_blocks = tile_owner[:, None] == jnp.arange(blocks, dtype=jnp.int32)[None, :]
        adjacency_matrix = jnp.where(select_blocks[:, None, :, None], tile_collection[:, :, None, :], jnp.zeros((), tiles.dtype)).reshape(TRAINER_SLOTS * BLOCK_NODE_ROWS, TRAINER_SEEDS)
        neighbour = jnp.dot(adjacency_matrix.T, messages, preferred_element_type=jnp.float32)
        own_rows = table[trainer][seed_local]
        summed = jnp.dot(own_rows, w_self, preferred_element_type=jnp.float32) + neighbour
        hidden = activate(summed).astype(jnp.bfloat16)
        _, pullback = jax.vjp(activate, summed)
        grad_pre = pullback(grad_local.astype(jnp.float32))[0].astype(jnp.bfloat16)
        grad_own = jnp.dot(own_rows.T, grad_pre, preferred_element_type=jnp.float32)
        grad_msg = jnp.dot(adjacency_matrix, grad_pre, preferred_element_type=jnp.float32).astype(jnp.bfloat16)
        grad_far = jnp.dot(neighbour_frontier.T, grad_msg, preferred_element_type=jnp.float32)
        return ((total_self + grad_own, total_neigh + grad_far), hidden)
    start_self = jnp.zeros((INPUT_WIDTH, H), jnp.float32)
    start_neigh = jnp.zeros((INPUT_WIDTH, H), jnp.float32)
    inputs = (owners, seed_view, request_rows, block_counts, tiles, tile_seed_block, grad_view)
    (grad_self, grad_neigh), hidden = lax.scan(per_trainer, (start_self, start_neigh), inputs)
    return (hidden.reshape(TRAINER_SEEDS * shards, H), grad_self, grad_neigh)
```

```python
import functools

import jax
import jax.numpy as jnp
from jax import lax
from jax.experimental import pallas as pl
from jax.experimental.pallas import tpu as pltpu
from jax.sharding import PartitionSpec as P

MESH = pl.DeviceIdType.MESH
BF16 = jnp.bfloat16
F32 = jnp.float32
LANES = 128
NZ, NX, NC = 4, 2, 2


def activate(values):
    return jax.nn.gelu(values, approximate=True)


def generic_body(
    features,
    seed_rows,
    request_rows,
    block_counts,
    tiles,
    tile_seed_block,
    w_self,
    w_neigh,
    grad_out,
):
    requests = request_rows[0]
    slot_count = requests.shape[1]
    feature_width = features.shape[1]
    usable = jnp.arange(slot_count, dtype=jnp.int32)[None, :] < block_counts[0][:, None]
    wanted = lax.all_to_all(
        jnp.where(usable[:, :, None], requests, -1), "shard", split_axis=0, concat_axis=0, tiled=True
    )
    selected_blocks = features[jnp.maximum(wanted, 0)]
    answered = lax.all_to_all(
        jnp.where(wanted[..., None] >= 0, selected_blocks, jnp.zeros((), features.dtype)),
        "shard",
        split_axis=0,
        concat_axis=0,
        tiled=True,
    )
    neighbour_frontier = answered.reshape(-1, feature_width)
    messages = jnp.dot(neighbour_frontier, w_neigh, preferred_element_type=F32).astype(BF16)
    seed_count = seed_rows.shape[0]
    block_rows = tiles.shape[3]
    blocks = seed_count // block_rows
    select_blocks = tile_seed_block[0][:, None] == jnp.arange(blocks, dtype=jnp.int32)[None, :]
    adjacency_matrix = jnp.where(
        select_blocks[:, None, :, None], tiles[0][:, :, None, :], jnp.zeros((), tiles.dtype)
    ).reshape(-1, seed_count)
    neighbour = jnp.dot(adjacency_matrix.T, messages, preferred_element_type=F32)
    own_rows = features[seed_rows]
    summed = jnp.dot(own_rows, w_self, preferred_element_type=F32) + neighbour
    hidden = activate(summed).astype(BF16)
    _, pullback = jax.vjp(activate, summed)
    grad_pre = pullback(grad_out.astype(F32))[0].astype(BF16)
    grad_self = lax.psum_scatter(
        jnp.dot(own_rows.T, grad_pre, preferred_element_type=F32),
        "shard",
        scatter_dimension=0,
        tiled=True,
    )
    grad_msg = jnp.dot(adjacency_matrix, grad_pre, preferred_element_type=F32).astype(BF16)
    grad_neigh = lax.psum_scatter(
        jnp.dot(neighbour_frontier.T, grad_msg, preferred_element_type=F32),
        "shard",
        scatter_dimension=0,
        tiled=True,
    )
    return (hidden, grad_self, grad_neigh)


def down_rows(row):
    return jnp.broadcast_to(row, (LANES, LANES)).T


def put_one_hot(oh, row, base, count):
    ids = down_rows(row)
    lane = lax.broadcasted_iota(jnp.int32, (LANES, LANES), 1)
    for c in range(count // LANES):
        oh[base : base + LANES, c * LANES : (c + 1) * LANES] = (
            (ids == lane + c * LANES).astype(F32).astype(BF16)
        )


def kernel(
    req_ref,
    ids_ref,
    tiles_ref,
    feat_hbm,
    ws_hbm,
    wn_hbm,
    go_hbm,
    hid_hbm,
    gs_ref,
    gn_ref,
    feat,
    ws,
    wn,
    gout,
    oh,
    reqs,
    ans,
    rows,
    adj,
    adjt,
    s,
    hid,
    rrows,
    at,
    bcat,
    bsend,
    xsend,
    xrecv,
    gk,
    zsend,
    zrecv,
    lsem,
    hsem,
    rq_s,
    rq_r,
    fr_s,
    fr_r,
    a_s,
    a_r,
    b_s,
    b_r,
    x_s,
    x_r,
    z_s,
    z_r,
):
    n = NZ * NX * NC
    me = lax.axis_index("shard")
    z, x, core = me // (NX * NC), (me // NC) % NX, me % NC
    half_n = n // 2
    near, far = me // half_n, 1 - me // half_n
    node_count, width = feat.shape
    per = ans.shape[2]
    nq, wq = hid.shape[0], hid.shape[2]
    seeds = hid.shape[1]

    def dev(zz, xx, cc):
        return {"shard": zz * (NX * NC) + xx * NC + cc}

    def z_xor(k):
        return (z, z + 1 - 2 * (z % 2), lax.rem(z + 2, NZ), NZ - 1 - z)[k]

    loads = [
        pltpu.make_async_copy(src, dst, lsem.at[i])
        for i, (src, dst) in enumerate(
            ((feat_hbm, feat), (ws_hbm, ws), (wn_hbm, wn), (go_hbm, gout))
        )
    ]
    for load in loads:
        load.start()
    barrier = pltpu.get_barrier_semaphore()
    others = [lax.rem(me + k, n) for k in range(1, n)]
    for other in others:
        pl.semaphore_signal(barrier, inc=1, device_id={"shard": other}, device_id_type=MESH)
    pl.semaphore_wait(barrier, n - 1)

    ask = []
    for k, owner in enumerate(others):
        ask.append(
            pltpu.make_async_remote_copy(
                src_ref=req_ref.at[owner],
                dst_ref=reqs.at[me],
                send_sem=rq_s.at[k],
                recv_sem=rq_r.at[me],
                device_id={"shard": owner},
                device_id_type=MESH,
            )
        )
        ask[-1].start()
    reqs[me] = req_ref[me]

    for h in range(seeds // LANES):
        put_one_hot(oh, ids_ref[h], h * LANES, node_count)
    loads[0].wait()
    for h in range(seeds // LANES):
        rows[h] = jnp.dot(
            oh[h * LANES : (h + 1) * LANES, :], feat[...], preferred_element_type=F32
        ).astype(BF16)

    lane = lax.broadcasted_iota(jnp.int32, (1, LANES), 1)
    answer = []
    for step, h in enumerate((far, near)):
        wanted = jnp.zeros((1, LANES), jnp.int32)
        for j in range(half_n):
            src = h * half_n + j

            @pl.when(src != me)
            def _():
                pltpu.make_async_remote_copy(
                    src_ref=reqs.at[src],
                    dst_ref=reqs.at[src],
                    send_sem=rq_s.at[0],
                    recv_sem=rq_r.at[src],
                    device_id={"shard": others[0]},
                    device_id_type=MESH,
                ).wait_recv()

            wanted = jnp.where(lane // per == j, reqs[src], wanted)
        put_one_hot(oh, wanted, 0, node_count)
        ans[h] = (
            jnp.dot(oh[0:LANES, :], feat[...], preferred_element_type=F32)
            .astype(BF16)
            .reshape(half_n, per, width)
        )
        mine = rows.at[2 + near, pl.ds(pl.multiple_of((me % half_n) * per, per), per)]
        for j in range(half_n):
            slot = lax.rem(me + j, half_n)
            dst = h * half_n + slot
            copy = pltpu.make_async_remote_copy(
                src_ref=ans.at[h, slot],
                dst_ref=mine,
                send_sem=fr_s.at[step, j],
                recv_sem=fr_r.at[me],
                device_id={"shard": dst},
                device_id_type=MESH,
            )
            if step == 1 and j == 0:
                own = pltpu.make_async_copy(ans.at[h, slot], mine, hsem.at[nq])
                own.start()
            else:
                copy.start()
                answer.append(copy)

    for h in range(2):
        seed_block = down_rows(ids_ref[2 + h])
        tile = tiles_ref[h * LANES : (h + 1) * LANES, :].astype(F32)
        for b in range(seeds // LANES):
            part = jnp.where(seed_block == b, tile, 0.0)
            adj[h * LANES : (h + 1) * LANES, b * LANES : (b + 1) * LANES] = part.astype(BF16)
            adjt[h, b * LANES : (b + 1) * LANES, :] = part.T.astype(BF16)
    loads[1].wait()
    own_rows = rows[0:2].reshape(seeds, width)
    for q in range(nq):
        s[q] = jnp.dot(own_rows, ws[:, q * wq : (q + 1) * wq], preferred_element_type=F32)
    loads[2].wait()
    loads[3].wait()

    def wait_rows(h, skip_me):
        for j in range(half_n):
            owner = h * half_n + j

            def wait():
                where = rows.at[2 + h, pl.ds(j * per, per)]
                pltpu.make_async_remote_copy(
                    src_ref=where,
                    dst_ref=where,
                    send_sem=fr_s.at[0, 0],
                    recv_sem=fr_r.at[owner],
                    device_id={"shard": others[0]},
                    device_id_type=MESH,
                ).wait_recv()

            if skip_me:
                pl.when(owner != me)(wait)
            else:
                wait()

    own.wait()
    wait_rows(near, True)
    for q in range(nq):
        msg = jnp.dot(
            rows[2 + near], wn[:, q * wq : (q + 1) * wq], preferred_element_type=F32
        ).astype(BF16)
        s[q] += jnp.dot(adjt[near], msg, preferred_element_type=F32)
    wait_rows(far, False)

    sibling = dev(z, x, 1 - core)
    trade_a = pltpu.make_async_remote_copy(
        src_ref=rows.at[pl.ds(2 * (1 - core), 2)],
        dst_ref=rrows,
        send_sem=a_s,
        recv_sem=a_r,
        device_id=sibling,
        device_id_type=MESH,
    )
    trade_a.start()
    trade_b, writes, xcopies, zcopies = [], [], [], []

    def seed_part(q):
        cols = slice(q * wq, (q + 1) * wq)
        msg = jnp.dot(rows[2 + far], wn[:, cols], preferred_element_type=F32).astype(BF16)
        v = s[q] + jnp.dot(adjt[far], msg, preferred_element_type=F32)
        c0 = 0.7978845608028654
        v2 = v * v
        t = jnp.tanh(c0 * v * (1.0 + 0.044715 * v2))
        cdf = 0.5 * (1.0 + t)
        hid[q] = (v * cdf).astype(BF16)
        slope = cdf + 0.5 * v * (1.0 - t * t) * (c0 * (1.0 + (3 * 0.044715) * v2))
        gp = (gout[:, cols].astype(F32) * slope).astype(BF16)
        gm = jnp.dot(adj[...], gp, preferred_element_type=F32).astype(BF16)

        @pl.when(core == 0)
        def _():
            bcat[q, 0:seeds, :] = gp
            bsend[q] = gm

        @pl.when(core != 0)
        def _():
            bcat[q, 0:seeds, :] = gm
            bsend[q] = gp

        copy = pltpu.make_async_remote_copy(
            src_ref=bsend.at[q],
            dst_ref=bcat.at[q, pl.ds(seeds, seeds)],
            send_sem=b_s.at[q],
            recv_sem=b_r.at[q],
            device_id=sibling,
            device_id_type=MESH,
        )
        copy.start()
        trade_b.append(copy)
        write = pltpu.make_async_copy(hid.at[q], hid_hbm.at[:, pl.ds(q * wq, wq)], hsem.at[q])
        write.start()
        writes.append(write)

    chip_rows = width // (NZ * NX)

    def put_transposed(values, at_col):
        turned = values.T
        for zz in range(NZ):
            for xx in range(NX):
                start = (zz * NX + xx) * chip_rows
                at[xx, zz * chip_rows : (zz + 1) * chip_rows, at_col : at_col + seeds] = turned[
                    start : start + chip_rows, :
                ]

    peer = dev(z, 1 - x, core)

    def x_part(q):
        trade_b[q].wait_recv()
        xsend[q] = (
            jnp.dot(at[1 - x], bcat[q], preferred_element_type=F32)
            .astype(BF16)
            .reshape(NZ, chip_rows, wq)
        )
        for k in range(NZ - 1, -1, -1):
            zb = z_xor(k)
            copy = pltpu.make_async_remote_copy(
                src_ref=xsend.at[q, zb],
                dst_ref=xrecv.at[q, zb],
                send_sem=x_s.at[q, k],
                recv_sem=x_r.at[q, k],
                device_id=peer,
                device_id_type=MESH,
            )
            copy.start()
            xcopies.append(copy)
        gk[q] = jnp.dot(at[x], bcat[q], preferred_element_type=F32).reshape(NZ, chip_rows, wq)

    def z_part(q):
        for k in range(NZ - 1, -1, -1):
            zb = z_xor(k)
            xcopies[q * NZ + NZ - 1 - k].wait_recv()
            total = gk[q, zb] + xrecv[q, zb].astype(F32)
            zsend[q, zb] = total.astype(BF16).reshape(NC, chip_rows // NC, wq)
            for i in range(NC):
                cc = 1 - core if i == 0 else core
                if k == 0 and i == 1:
                    zrecv[q, core, z] = zsend[q, z, core]
                    continue
                copy = pltpu.make_async_remote_copy(
                    src_ref=zsend.at[q, zb, cc],
                    dst_ref=zrecv.at[q, core, z],
                    send_sem=z_s.at[q, k, i],
                    recv_sem=z_r.at[q, core, z],
                    device_id=dev(zb, x, cc),
                    device_id_type=MESH,
                )
                copy.start()
                zcopies.append(copy)

    def last_part(q):
        for i in range(NC):
            for k in range(NZ):
                if i == 0 and k == 0:
                    continue
                g = core if i == 0 else 1 - core
                where = zrecv.at[q, g, z_xor(k)]
                pltpu.make_async_remote_copy(
                    src_ref=where,
                    dst_ref=where,
                    send_sem=z_s.at[0, 0, 0],
                    recv_sem=z_r.at[q, g, z_xor(k)],
                    device_id=sibling,
                    device_id_type=MESH,
                ).wait_recv()
        for g, out in enumerate((gs_ref, gn_ref)):
            parts = zrecv[q, g].astype(F32)
            out[:, q * wq : (q + 1) * wq] = (parts[0] + parts[1]) + (parts[2] + parts[3])

    seed_part(0)
    put_transposed(rows[pl.ds(2 * core, 2)].reshape(seeds, width), 0)
    seed_part(1)
    trade_a.wait_recv()
    put_transposed(rrows[...].reshape(seeds, width), seeds)
    x_part(0)
    for q in range(2, nq):
        seed_part(q)
        x_part(q - 1)
    x_part(nq - 1)
    for q in range(nq):
        z_part(q)
    for q in range(nq):
        last_part(q)
    for copy in ask + answer + [trade_a] + trade_b + xcopies + zcopies:
        copy.wait_send()
    for write in writes:
        write.wait()


def kernel_body(
    features,
    seed_rows,
    request_rows,
    block_counts,
    tiles,
    tile_seed_block,
    w_self,
    w_neigh,
    grad_out,
):
    n, cap, block = request_rows.shape[1:]
    per = cap * block
    node_count, width = features.shape
    seeds, hidden_width = grad_out.shape
    usable = jnp.arange(cap, dtype=jnp.int32)[None, :] < block_counts[0][:, None]
    wanted = jnp.where(usable[:, :, None], request_rows[0], -1).reshape(n, 1, per)
    wanted = jnp.tile(wanted, (1, 1, LANES // per))
    ids = jnp.concatenate([seed_rows, jnp.repeat(tile_seed_block[0], block)]).reshape(4, 1, LANES)
    nq = 4
    wq = hidden_width // nq
    chip_rows = width // (NZ * NX)
    out_rows = width // n
    vmem = pl.BlockSpec(memory_space=pltpu.VMEM)
    hbm = pl.BlockSpec(memory_space=pl.ANY)
    dma = pltpu.SemaphoreType.DMA
    return pl.pallas_call(
        kernel,
        out_shape=(
            jax.ShapeDtypeStruct((seeds, hidden_width), BF16),
            jax.ShapeDtypeStruct((out_rows, hidden_width), F32),
            jax.ShapeDtypeStruct((out_rows, hidden_width), F32),
        ),
        in_specs=[vmem] * 3 + [hbm] * 4,
        out_specs=(hbm, vmem, vmem),
        scratch_shapes=[
            pltpu.VMEM((node_count, width), BF16),
            pltpu.VMEM((width, hidden_width), BF16),
            pltpu.VMEM((width, hidden_width), BF16),
            pltpu.VMEM((seeds, hidden_width), BF16),
            pltpu.VMEM((seeds, node_count), BF16),
            pltpu.VMEM((n, 1, LANES), jnp.int32),
            pltpu.VMEM((2, n // 2, per, width), BF16),
            pltpu.VMEM((4, LANES, width), BF16),
            pltpu.VMEM((seeds, seeds), BF16),
            pltpu.VMEM((2, seeds, LANES), BF16),
            pltpu.VMEM((nq, seeds, wq), F32),
            pltpu.VMEM((nq, seeds, wq), BF16),
            pltpu.VMEM((2, LANES, width), BF16),
            pltpu.VMEM((NX, NZ * chip_rows, 2 * seeds), BF16),
            pltpu.VMEM((nq, 2 * seeds, wq), BF16),
            pltpu.VMEM((nq, seeds, wq), BF16),
            pltpu.VMEM((nq, NZ, chip_rows, wq), BF16),
            pltpu.VMEM((nq, NZ, chip_rows, wq), BF16),
            pltpu.VMEM((nq, NZ, chip_rows, wq), F32),
            pltpu.VMEM((nq, NZ, NC, out_rows, wq), BF16),
            pltpu.VMEM((nq, NC, NZ, out_rows, wq), BF16),
            dma((4,)),
            dma((nq + 1,)),
            dma((n - 1,)),
            dma((n,)),
            dma((2, n // 2)),
            dma((n,)),
            dma,
            dma,
            dma((nq,)),
            dma((nq,)),
            dma((nq, NZ)),
            dma((nq, NZ)),
            dma((nq, NZ, NC)),
            dma((nq, NC, NZ)),
        ],
        compiler_params=pltpu.CompilerParams(
            collective_id=0, has_side_effects=True, vmem_limit_bytes=48 * 1024 * 1024
        ),
        name="layer_step",
    )(
        wanted,
        ids,
        tiles.reshape(-1, tiles.shape[3]),
        features,
        w_self,
        w_neigh,
        grad_out,
    )


def solution(mesh):
    in_specs = (
        P("shard", None),
        P(("group", "shard")),
        P(("group", "shard"), None, None, None),
        P(("group", "shard"), None),
        P(("group", "shard"), None, None, None),
        P(("group", "shard"), None),
        P(),
        P(),
        P(("group", "shard"), None),
    )
    out_specs = (
        P(("group", "shard"), None),
        P(("group", "shard"), None),
        P(("group", "shard"), None),
    )
    body = kernel_body if mesh.shape["shard"] == NZ * NX * NC else generic_body
    return jax.shard_map(body, mesh=mesh, in_specs=in_specs, out_specs=out_specs, check_vma=False)
```

```python
import functools

import jax
import jax.numpy as jnp
from jax import lax
from jax.experimental import pallas as pl
from jax.experimental.pallas import tpu as pltpu
from jax.sharding import PartitionSpec as P

MESH = pl.DeviceIdType.MESH
BF16 = jnp.bfloat16
F32 = jnp.float32
LANES = 128
NZ, NX, NC = 4, 2, 2


def activate(values):
    return jax.nn.gelu(values, approximate=True)


def generic_body(
    features,
    seed_rows,
    request_rows,
    block_counts,
    tiles,
    tile_seed_block,
    w_self,
    w_neigh,
    grad_out,
):
    requests = request_rows[0]
    slot_count = requests.shape[1]
    feature_width = features.shape[1]
    usable = jnp.arange(slot_count, dtype=jnp.int32)[None, :] < block_counts[0][:, None]
    wanted = lax.all_to_all(
        jnp.where(usable[:, :, None], requests, -1), "shard", split_axis=0, concat_axis=0, tiled=True
    )
    selected_blocks = features[jnp.maximum(wanted, 0)]
    answered = lax.all_to_all(
        jnp.where(wanted[..., None] >= 0, selected_blocks, jnp.zeros((), features.dtype)),
        "shard",
        split_axis=0,
        concat_axis=0,
        tiled=True,
    )
    neighbour_frontier = answered.reshape(-1, feature_width)
    messages = jnp.dot(neighbour_frontier, w_neigh, preferred_element_type=F32).astype(BF16)
    seed_count = seed_rows.shape[0]
    block_rows = tiles.shape[3]
    blocks = seed_count // block_rows
    select_blocks = tile_seed_block[0][:, None] == jnp.arange(blocks, dtype=jnp.int32)[None, :]
    adjacency_matrix = jnp.where(
        select_blocks[:, None, :, None], tiles[0][:, :, None, :], jnp.zeros((), tiles.dtype)
    ).reshape(-1, seed_count)
    neighbour = jnp.dot(adjacency_matrix.T, messages, preferred_element_type=F32)
    own_rows = features[seed_rows]
    summed = jnp.dot(own_rows, w_self, preferred_element_type=F32) + neighbour
    hidden = activate(summed).astype(BF16)
    _, pullback = jax.vjp(activate, summed)
    grad_pre = pullback(grad_out.astype(F32))[0].astype(BF16)
    grad_self = lax.psum_scatter(
        jnp.dot(own_rows.T, grad_pre, preferred_element_type=F32),
        "shard",
        scatter_dimension=0,
        tiled=True,
    )
    grad_msg = jnp.dot(adjacency_matrix, grad_pre, preferred_element_type=F32).astype(BF16)
    grad_neigh = lax.psum_scatter(
        jnp.dot(neighbour_frontier.T, grad_msg, preferred_element_type=F32),
        "shard",
        scatter_dimension=0,
        tiled=True,
    )
    return (hidden, grad_self, grad_neigh)


def down_rows(row):
    return jnp.broadcast_to(row, (LANES, LANES)).T


def put_one_hot(oh, ids, base, count):
    lane = lax.broadcasted_iota(jnp.int32, (LANES, LANES), 1)
    for c in range(count // LANES):
        oh[base : base + LANES, c * LANES : (c + 1) * LANES] = (
            (ids == lane + c * LANES).astype(F32).astype(BF16)
        )


def kernel(
    counts_ref,
    block_ref,
    wanted_ref,
    seeds_ref,
    tiles_ref,
    feat_hbm,
    ws_hbm,
    wn_hbm,
    go_hbm,
    hid_hbm,
    gs_ref,
    gn_ref,
    feat,
    ws,
    wn,
    gout,
    oh,
    turn,
    req_ref,
    reqs,
    ans,
    rows,
    adj32,
    adj,
    adjt,
    s,
    hid,
    rrows,
    at,
    bcat,
    bsend,
    xsend,
    xrecv,
    gk,
    zsend,
    zrecv,
    lsem,
    hsem,
    rq_s,
    rq_r,
    fr_s,
    fr_r,
    a_s,
    a_r,
    b_s,
    b_r,
    x_s,
    x_r,
    z_s,
    z_r,
):
    n = NZ * NX * NC
    me = lax.axis_index("shard")
    z, x, core = me // (NX * NC), (me // NC) % NX, me % NC
    half_n = n // 2
    near, far = me // half_n, 1 - me // half_n
    node_count, width = feat.shape
    per = ans.shape[2]
    nq, wq = hid.shape[0], hid.shape[2]
    seeds = hid.shape[1]

    def dev(zz, xx, cc):
        return {"shard": zz * (NX * NC) + xx * NC + cc}

    def z_xor(k):
        return (z, z + 1 - 2 * (z % 2), lax.rem(z + 2, NZ), NZ - 1 - z)[k]

    loads = [
        pltpu.make_async_copy(src, dst, lsem.at[i])
        for i, (src, dst) in enumerate(
            ((feat_hbm, feat), (ws_hbm, ws), (wn_hbm, wn), (go_hbm, gout))
        )
    ]
    for load in loads:
        load.start()
    barrier = pltpu.get_barrier_semaphore()
    others = [lax.rem(me + k, n) for k in range(1, n)]
    for other in others:
        pl.semaphore_signal(barrier, inc=1, device_id={"shard": other}, device_id_type=MESH)
    cap, block = wanted_ref.shape[:2]
    for j in range(cap):
        turn[j * block : (j + 1) * block, 0:n] = jnp.where(
            j < counts_ref[...], wanted_ref[j], -1
        )
    turned = turn[...].T
    for owner in range(n):
        req_ref[owner] = turned[owner : owner + 1, :]
    pl.semaphore_wait(barrier, n - 1)

    ask = []
    for k, owner in enumerate(others):
        ask.append(
            pltpu.make_async_remote_copy(
                src_ref=req_ref.at[owner],
                dst_ref=reqs.at[me],
                send_sem=rq_s.at[k],
                recv_sem=rq_r.at[me],
                device_id={"shard": owner},
                device_id_type=MESH,
            )
        )
        ask[-1].start()
    reqs[me] = req_ref[me]

    for h in range(seeds // LANES):
        put_one_hot(oh, down_rows(seeds_ref[h : h + 1, :]), h * LANES, node_count)
    loads[0].wait()
    for h in range(seeds // LANES):
        rows[h] = jnp.dot(
            oh[h * LANES : (h + 1) * LANES, :], feat[...], preferred_element_type=F32
        ).astype(BF16)

    answer = []
    for step, h in enumerate((far, near)):
        for j in range(half_n):
            src = h * half_n + j

            @pl.when(src != me)
            def _():
                pltpu.make_async_remote_copy(
                    src_ref=reqs.at[src],
                    dst_ref=reqs.at[src],
                    send_sem=rq_s.at[0],
                    recv_sem=rq_r.at[src],
                    device_id={"shard": others[0]},
                    device_id_type=MESH,
                ).wait_recv()
            turn[j : j + 1, :] = reqs[src]
        turned = turn[...].T
        wanted = [
            jnp.broadcast_to(turned[0:per, j : j + 1], (per, LANES)) for j in range(half_n)
        ]
        put_one_hot(oh, jnp.concatenate(wanted, axis=0), 0, node_count)
        ans[h] = (
            jnp.dot(oh[0:LANES, :], feat[...], preferred_element_type=F32)
            .astype(BF16)
            .reshape(half_n, per, width)
        )
        mine = rows.at[2 + near, pl.ds(pl.multiple_of((me % half_n) * per, per), per)]
        for j in range(half_n):
            slot = lax.rem(me + j, half_n)
            dst = h * half_n + slot
            if step == 1 and j == 0:
                own = pltpu.make_async_copy(ans.at[h, slot], mine, hsem.at[nq])
                own.start()
                continue
            copy = pltpu.make_async_remote_copy(
                src_ref=ans.at[h, slot],
                dst_ref=mine,
                send_sem=fr_s.at[step, j],
                recv_sem=fr_r.at[me],
                device_id={"shard": dst},
                device_id_type=MESH,
            )
            copy.start()
            answer.append(copy)

    for slot in range(tiles_ref.shape[0]):
        tile = tiles_ref[slot].astype(F32)
        for b in range(seeds // LANES):
            adj32[slot * block : (slot + 1) * block, b * LANES : (b + 1) * LANES] = jnp.where(
                block_ref[0, slot] == b, tile, 0.0
            )
    adj[...] = adj32[...].astype(BF16)
    for h in range(2):
        adjt[h] = adj32[h * LANES : (h + 1) * LANES, :].T.astype(BF16)
    loads[1].wait()
    own_rows = rows[0:2].reshape(seeds, width)
    for q in range(nq):
        s[q] = jnp.dot(own_rows, ws[:, q * wq : (q + 1) * wq], preferred_element_type=F32)
    loads[2].wait()
    loads[3].wait()

    def wait_rows(h, skip_me):
        for j in range(half_n):
            owner = h * half_n + j

            def wait():
                where = rows.at[2 + h, pl.ds(j * per, per)]
                pltpu.make_async_remote_copy(
                    src_ref=where,
                    dst_ref=where,
                    send_sem=fr_s.at[0, 0],
                    recv_sem=fr_r.at[owner],
                    device_id={"shard": others[0]},
                    device_id_type=MESH,
                ).wait_recv()

            if skip_me:
                pl.when(owner != me)(wait)
            else:
                wait()

    own.wait()
    wait_rows(near, True)
    for q in range(nq):
        msg = jnp.dot(
            rows[2 + near], wn[:, q * wq : (q + 1) * wq], preferred_element_type=F32
        ).astype(BF16)
        s[q] += jnp.dot(adjt[near], msg, preferred_element_type=F32)
    wait_rows(far, False)

    sibling = dev(z, x, 1 - core)
    trade_a = pltpu.make_async_remote_copy(
        src_ref=rows.at[pl.ds(2 * (1 - core), 2)],
        dst_ref=rrows,
        send_sem=a_s,
        recv_sem=a_r,
        device_id=sibling,
        device_id_type=MESH,
    )
    trade_a.start()
    trade_b, writes, xcopies, zcopies = [], [], [], []

    def seed_part(q):
        cols = slice(q * wq, (q + 1) * wq)
        msg = jnp.dot(rows[2 + far], wn[:, cols], preferred_element_type=F32).astype(BF16)
        v = s[q] + jnp.dot(adjt[far], msg, preferred_element_type=F32)
        c0 = 0.7978845608028654
        v2 = v * v
        t = jnp.tanh(c0 * v * (1.0 + 0.044715 * v2))
        cdf = 0.5 * (1.0 + t)
        hid[q] = (v * cdf).astype(BF16)
        slope = cdf + 0.5 * v * (1.0 - t * t) * (c0 * (1.0 + (3 * 0.044715) * v2))
        gp = (gout[:, cols].astype(F32) * slope).astype(BF16)
        gm = jnp.dot(adj[...], gp, preferred_element_type=F32).astype(BF16)

        @pl.when(core == 0)
        def _():
            bcat[q, 0:seeds, :] = gp
            bsend[q] = gm

        @pl.when(core != 0)
        def _():
            bcat[q, 0:seeds, :] = gm
            bsend[q] = gp

        copy = pltpu.make_async_remote_copy(
            src_ref=bsend.at[q],
            dst_ref=bcat.at[q, pl.ds(seeds, seeds)],
            send_sem=b_s.at[q],
            recv_sem=b_r.at[q],
            device_id=sibling,
            device_id_type=MESH,
        )
        copy.start()
        trade_b.append(copy)
        write = pltpu.make_async_copy(hid.at[q], hid_hbm.at[:, pl.ds(q * wq, wq)], hsem.at[q])
        write.start()
        writes.append(write)

    chip_rows = width // (NZ * NX)

    def put_transposed(values, at_col):
        turned = values.T
        for zz in range(NZ):
            for xx in range(NX):
                start = (zz * NX + xx) * chip_rows
                at[xx, zz * chip_rows : (zz + 1) * chip_rows, at_col : at_col + seeds] = turned[
                    start : start + chip_rows, :
                ]

    peer = dev(z, 1 - x, core)

    def x_part(q):
        trade_b[q].wait_recv()
        xsend[q] = (
            jnp.dot(at[1 - x], bcat[q], preferred_element_type=F32)
            .astype(BF16)
            .reshape(NZ, chip_rows, wq)
        )
        for k in range(NZ - 1, -1, -1):
            zb = z_xor(k)
            copy = pltpu.make_async_remote_copy(
                src_ref=xsend.at[q, zb],
                dst_ref=xrecv.at[q, zb],
                send_sem=x_s.at[q, k],
                recv_sem=x_r.at[q, k],
                device_id=peer,
                device_id_type=MESH,
            )
            copy.start()
            xcopies.append(copy)
        gk[q] = jnp.dot(at[x], bcat[q], preferred_element_type=F32).reshape(NZ, chip_rows, wq)

    def z_part(q):
        for k in range(NZ - 1, -1, -1):
            zb = z_xor(k)
            xcopies[q * NZ + NZ - 1 - k].wait_recv()
            total = gk[q, zb] + xrecv[q, zb].astype(F32)
            zsend[q, zb] = total.astype(BF16).reshape(NC, chip_rows // NC, wq)
            for i in range(NC):
                cc = 1 - core if i == 0 else core
                if k == 0 and i == 1:
                    zrecv[q, core, z] = zsend[q, z, core]
                    continue
                copy = pltpu.make_async_remote_copy(
                    src_ref=zsend.at[q, zb, cc],
                    dst_ref=zrecv.at[q, core, z],
                    send_sem=z_s.at[q, k, i],
                    recv_sem=z_r.at[q, core, z],
                    device_id=dev(zb, x, cc),
                    device_id_type=MESH,
                )
                copy.start()
                zcopies.append(copy)

    def last_part(q):
        for i in range(NC):
            for k in range(NZ):
                if i == 0 and k == 0:
                    continue
                g = core if i == 0 else 1 - core
                where = zrecv.at[q, g, z_xor(k)]
                pltpu.make_async_remote_copy(
                    src_ref=where,
                    dst_ref=where,
                    send_sem=z_s.at[0, 0, 0],
                    recv_sem=z_r.at[q, g, z_xor(k)],
                    device_id=sibling,
                    device_id_type=MESH,
                ).wait_recv()
        for g, out in enumerate((gs_ref, gn_ref)):
            parts = zrecv[q, g].astype(F32)
            out[:, q * wq : (q + 1) * wq] = (parts[0] + parts[1]) + (parts[2] + parts[3])

    seed_part(0)
    put_transposed(rows[pl.ds(2 * core, 2)].reshape(seeds, width), 0)
    seed_part(1)
    trade_a.wait_recv()
    put_transposed(rrows[...].reshape(seeds, width), seeds)
    x_part(0)
    for q in range(2, nq):
        seed_part(q)
        x_part(q - 1)
    x_part(nq - 1)
    for q in range(nq):
        z_part(q)
    for q in range(nq):
        last_part(q)
    for copy in ask + answer + [trade_a] + trade_b + xcopies + zcopies:
        copy.wait_send()
    for write in writes:
        write.wait()


def kernel_body(
    features,
    seed_rows,
    request_rows,
    block_counts,
    tiles,
    tile_seed_block,
    w_self,
    w_neigh,
    grad_out,
):
    n, cap, block = request_rows.shape[1:]
    per = cap * block
    node_count, width = features.shape
    seeds, hidden_width = grad_out.shape
    nq = 4
    wq = hidden_width // nq
    chip_rows = width // (NZ * NX)
    out_rows = width // n
    vmem = pl.BlockSpec(memory_space=pltpu.VMEM)
    smem = pl.BlockSpec(memory_space=pltpu.SMEM)
    hbm = pl.BlockSpec(memory_space=pltpu.HBM)
    dma = pltpu.SemaphoreType.DMA
    results = pl.pallas_call(
        kernel,
        out_shape=(
            jax.ShapeDtypeStruct((seeds, hidden_width), BF16),
            jax.ShapeDtypeStruct((out_rows, hidden_width), F32),
            jax.ShapeDtypeStruct((out_rows, hidden_width), F32),
        ),
        in_specs=[vmem, smem] + [vmem] * 3 + [hbm] * 4,
        out_specs=(hbm, vmem, vmem),
        scratch_shapes=[
            pltpu.VMEM((node_count, width), BF16),
            pltpu.VMEM((width, hidden_width), BF16),
            pltpu.VMEM((width, hidden_width), BF16),
            pltpu.VMEM((seeds, hidden_width), BF16),
            pltpu.VMEM((seeds, node_count), BF16),
            pltpu.VMEM((LANES, LANES), jnp.int32),
            pltpu.VMEM((n, 1, LANES), jnp.int32),
            pltpu.VMEM((n, 1, LANES), jnp.int32),
            pltpu.VMEM((2, n // 2, per, width), BF16),
            pltpu.VMEM((4, LANES, width), BF16),
            pltpu.VMEM((seeds, seeds), F32),
            pltpu.VMEM((seeds, seeds), BF16),
            pltpu.VMEM((2, seeds, LANES), BF16),
            pltpu.VMEM((nq, seeds, wq), F32),
            pltpu.VMEM((nq, seeds, wq), BF16),
            pltpu.VMEM((2, LANES, width), BF16),
            pltpu.VMEM((NX, NZ * chip_rows, 2 * seeds), BF16),
            pltpu.VMEM((nq, 2 * seeds, wq), BF16),
            pltpu.VMEM((nq, seeds, wq), BF16),
            pltpu.VMEM((nq, NZ, chip_rows, wq), BF16),
            pltpu.VMEM((nq, NZ, chip_rows, wq), BF16),
            pltpu.VMEM((nq, NZ, chip_rows, wq), F32),
            pltpu.VMEM((nq, NZ, NC, out_rows, wq), BF16),
            pltpu.VMEM((nq, NC, NZ, out_rows, wq), BF16),
            dma((4,)),
            dma((nq + 1,)),
            dma((n - 1,)),
            dma((n,)),
            dma((2, n // 2)),
            dma((n,)),
            dma,
            dma,
            dma((nq,)),
            dma((nq,)),
            dma((nq, NZ)),
            dma((nq, NZ)),
            dma((nq, NZ, NC)),
            dma((nq, NC, NZ)),
        ],
        compiler_params=pltpu.CompilerParams(
            collective_id=0, has_side_effects=True, vmem_limit_bytes=62 * 1024 * 1024
        ),
        name="layer_step",
    )(
        block_counts,
        tile_seed_block,
        jnp.transpose(request_rows[0], (1, 2, 0)),
        seed_rows.reshape(-1, LANES),
        tiles[0],
        features,
        w_self,
        w_neigh,
        grad_out,
    )
    return pl.pallas_call(
        hand_out,
        out_shape=tuple(jax.ShapeDtypeStruct(r.shape, r.dtype) for r in results),
        in_specs=[hbm] * 3,
        out_specs=(hbm,) * 3,
        scratch_shapes=[dma((3,))],
        name="hand_out",
    )(*results)


def hand_out(a_ref, b_ref, c_ref, a_out, b_out, c_out, sem):
    copies = [
        pltpu.make_async_copy(src, dst, sem.at[i])
        for i, (src, dst) in enumerate(((a_ref, a_out), (b_ref, b_out), (c_ref, c_out)))
    ]
    for copy in copies:
        copy.start()
    for copy in copies:
        copy.wait()


def solution(mesh):
    in_specs = (
        P("shard", None),
        P(("group", "shard")),
        P(("group", "shard"), None, None, None),
        P(("group", "shard"), None),
        P(("group", "shard"), None, None, None),
        P(("group", "shard"), None),
        P(),
        P(),
        P(("group", "shard"), None),
    )
    out_specs = (
        P(("group", "shard"), None),
        P(("group", "shard"), None),
        P(("group", "shard"), None),
    )
    body = kernel_body if mesh.shape["shard"] == NZ * NX * NC else generic_body
    return jax.shard_map(body, mesh=mesh, in_specs=in_specs, out_specs=out_specs, check_vma=False)
```

```python
import functools

import jax
import jax.numpy as jnp
from jax import lax
from jax.experimental import pallas as pl
from jax.experimental.pallas import tpu as pltpu
from jax.sharding import PartitionSpec as P

MESH = pl.DeviceIdType.MESH
BF16 = jnp.bfloat16
F32 = jnp.float32
LANES = 128
NZ, NX, NC = 4, 2, 2


def activate(values):
    return jax.nn.gelu(values, approximate=True)


def generic_body(
    features,
    seed_rows,
    request_rows,
    block_counts,
    tiles,
    tile_seed_block,
    w_self,
    w_neigh,
    grad_out,
):
    requests = request_rows[0]
    slot_count = requests.shape[1]
    feature_width = features.shape[1]
    usable = jnp.arange(slot_count, dtype=jnp.int32)[None, :] < block_counts[0][:, None]
    wanted = lax.all_to_all(
        jnp.where(usable[:, :, None], requests, -1), "shard", split_axis=0, concat_axis=0, tiled=True
    )
    selected_blocks = features[jnp.maximum(wanted, 0)]
    answered = lax.all_to_all(
        jnp.where(wanted[..., None] >= 0, selected_blocks, jnp.zeros((), features.dtype)),
        "shard",
        split_axis=0,
        concat_axis=0,
        tiled=True,
    )
    neighbour_frontier = answered.reshape(-1, feature_width)
    messages = jnp.dot(neighbour_frontier, w_neigh, preferred_element_type=F32).astype(BF16)
    seed_count = seed_rows.shape[0]
    block_rows = tiles.shape[3]
    blocks = seed_count // block_rows
    select_blocks = tile_seed_block[0][:, None] == jnp.arange(blocks, dtype=jnp.int32)[None, :]
    adjacency_matrix = jnp.where(
        select_blocks[:, None, :, None], tiles[0][:, :, None, :], jnp.zeros((), tiles.dtype)
    ).reshape(-1, seed_count)
    neighbour = jnp.dot(adjacency_matrix.T, messages, preferred_element_type=F32)
    own_rows = features[seed_rows]
    summed = jnp.dot(own_rows, w_self, preferred_element_type=F32) + neighbour
    hidden = activate(summed).astype(BF16)
    _, pullback = jax.vjp(activate, summed)
    grad_pre = pullback(grad_out.astype(F32))[0].astype(BF16)
    grad_self = lax.psum_scatter(
        jnp.dot(own_rows.T, grad_pre, preferred_element_type=F32),
        "shard",
        scatter_dimension=0,
        tiled=True,
    )
    grad_msg = jnp.dot(adjacency_matrix, grad_pre, preferred_element_type=F32).astype(BF16)
    grad_neigh = lax.psum_scatter(
        jnp.dot(neighbour_frontier.T, grad_msg, preferred_element_type=F32),
        "shard",
        scatter_dimension=0,
        tiled=True,
    )
    return (hidden, grad_self, grad_neigh)


def down_rows(row):
    return jnp.broadcast_to(row, (LANES, LANES)).T


def put_one_hot(oh, ids, base, count):
    lane = lax.broadcasted_iota(jnp.int32, (LANES, LANES), 1)
    for c in range(count // LANES):
        oh[base : base + LANES, c * LANES : (c + 1) * LANES] = (
            (ids == lane + c * LANES).astype(F32).astype(BF16)
        )


def kernel(
    counts_ref,
    block_ref,
    wanted_ref,
    seeds_ref,
    tiles_ref,
    feat_hbm,
    ws_hbm,
    wn_hbm,
    go_hbm,
    hid_hbm,
    gs_hbm,
    gn_hbm,
    feat,
    ws,
    wn,
    gout,
    oh,
    turn,
    req_ref,
    reqs,
    ans,
    rows,
    adj32,
    adj,
    adjt,
    s,
    hid,
    gs,
    gn,
    turned_rows,
    recv_turned,
    bcat,
    bsend,
    xsend,
    xrecv,
    gk,
    zsend,
    zrecv,
    lsem,
    hsem,
    osem,
    rq_s,
    rq_r,
    fr_s,
    fr_r,
    a_s,
    a_r,
    b_s,
    b_r,
    x_s,
    x_r,
    z_s,
    z_r,
):
    n = NZ * NX * NC
    me = lax.axis_index("shard")
    z, x, core = me // (NX * NC), (me // NC) % NX, me % NC
    half_n = n // 2
    near, far = me // half_n, 1 - me // half_n
    node_count, width = feat.shape
    per = ans.shape[2]
    nq, wq = hid.shape[0], hid.shape[2]
    seeds = hid.shape[1]

    def dev(zz, xx, cc):
        return {"shard": zz * (NX * NC) + xx * NC + cc}

    def z_xor(k):
        return (z, z + 1 - 2 * (z % 2), lax.rem(z + 2, NZ), NZ - 1 - z)[k]

    loads = [
        pltpu.make_async_copy(src, dst, lsem.at[i])
        for i, (src, dst) in enumerate(
            ((feat_hbm, feat), (ws_hbm, ws), (wn_hbm, wn), (go_hbm, gout))
        )
    ]
    for load in loads:
        load.start()
    barrier = pltpu.get_barrier_semaphore()
    others = [lax.rem(me + k, n) for k in range(1, n)]
    for other in others:
        pl.semaphore_signal(barrier, inc=1, device_id={"shard": other}, device_id_type=MESH)
    cap, block = wanted_ref.shape[:2]
    for j in range(cap):
        turn[j * block : (j + 1) * block, 0:n] = jnp.where(
            j < counts_ref[...], wanted_ref[j], -1
        )
    turned = turn[...].T
    for owner in range(n):
        req_ref[owner] = turned[owner : owner + 1, :]
    pl.semaphore_wait(barrier, n - 1)

    chip_rows = width // (NZ * NX)

    def put_turned(kind, h):
        turned = rows[2 * kind + h].T
        lanes = pl.ds(pl.multiple_of(h * LANES, LANES), LANES)
        for zz in range(NZ):
            for xx in range(NX):
                start = (zz * NX + xx) * chip_rows
                turned_rows[kind, xx, zz * chip_rows : (zz + 1) * chip_rows, lanes] = turned[
                    start : start + chip_rows, :
                ]

    ask = []
    for k, owner in enumerate(others):
        ask.append(
            pltpu.make_async_remote_copy(
                src_ref=req_ref.at[owner],
                dst_ref=reqs.at[me],
                send_sem=rq_s.at[k],
                recv_sem=rq_r.at[me],
                device_id={"shard": owner},
                device_id_type=MESH,
            )
        )
        ask[-1].start()
    reqs[me] = req_ref[me]

    answer = []
    for step, h in enumerate((far, near)):
        for j in range(half_n):
            src = h * half_n + j

            @pl.when(src != me)
            def _():
                pltpu.make_async_remote_copy(
                    src_ref=reqs.at[src],
                    dst_ref=reqs.at[src],
                    send_sem=rq_s.at[0],
                    recv_sem=rq_r.at[src],
                    device_id={"shard": others[0]},
                    device_id_type=MESH,
                ).wait_recv()
            turn[j : j + 1, :] = reqs[src]
        turned = turn[...].T
        wanted = [
            jnp.broadcast_to(turned[0:per, j : j + 1], (per, LANES)) for j in range(half_n)
        ]
        put_one_hot(oh, jnp.concatenate(wanted, axis=0), 0, node_count)
        if step == 0:
            loads[0].wait()
        ans[h] = (
            jnp.dot(oh[0:LANES, :], feat[...], preferred_element_type=F32)
            .astype(BF16)
            .reshape(half_n, per, width)
        )
        mine = rows.at[2 + near, pl.ds(pl.multiple_of((me % half_n) * per, per), per)]
        for j in range(half_n):
            slot = lax.rem(me + j, half_n)
            dst = h * half_n + slot
            if step == 1 and j == 0:
                own = pltpu.make_async_copy(ans.at[h, slot], mine, hsem.at[nq])
                own.start()
                continue
            copy = pltpu.make_async_remote_copy(
                src_ref=ans.at[h, slot],
                dst_ref=mine,
                send_sem=fr_s.at[step, j],
                recv_sem=fr_r.at[me],
                device_id={"shard": dst},
                device_id_type=MESH,
            )
            copy.start()
            answer.append(copy)

    for h in range(seeds // LANES):
        put_one_hot(oh, down_rows(seeds_ref[h : h + 1, :]), h * LANES, node_count)
    for h in range(seeds // LANES):
        rows[h] = jnp.dot(
            oh[h * LANES : (h + 1) * LANES, :], feat[...], preferred_element_type=F32
        ).astype(BF16)

    for slot in range(tiles_ref.shape[0]):
        tile = tiles_ref[slot].astype(F32)
        for b in range(seeds // LANES):
            adj32[slot * block : (slot + 1) * block, b * LANES : (b + 1) * LANES] = jnp.where(
                block_ref[0, slot] == b, tile, 0.0
            )
    adj[...] = adj32[...].astype(BF16)
    for h in range(2):
        adjt[h] = adj32[h * LANES : (h + 1) * LANES, :].T.astype(BF16)
    loads[1].wait()
    own_rows = rows[0:2].reshape(seeds, width)
    for q in range(nq):
        s[q] = jnp.dot(own_rows, ws[:, q * wq : (q + 1) * wq], preferred_element_type=F32)
    loads[2].wait()
    loads[3].wait()

    def wait_rows(h, skip_me):
        for j in range(half_n):
            owner = h * half_n + j

            def wait():
                where = rows.at[2 + h, pl.ds(j * per, per)]
                pltpu.make_async_remote_copy(
                    src_ref=where,
                    dst_ref=where,
                    send_sem=fr_s.at[0, 0],
                    recv_sem=fr_r.at[owner],
                    device_id={"shard": others[0]},
                    device_id_type=MESH,
                ).wait_recv()

            if skip_me:
                pl.when(owner != me)(wait)
            else:
                wait()

    put_turned(0, 0)
    put_turned(0, 1)
    own.wait()
    wait_rows(near, True)
    put_turned(1, near)
    for q in range(nq):
        msg = jnp.dot(
            rows[2 + near], wn[:, q * wq : (q + 1) * wq], preferred_element_type=F32
        ).astype(BF16)
        s[q] += jnp.dot(adjt[near], msg, preferred_element_type=F32)
    wait_rows(far, False)
    put_turned(1, far)

    sibling = dev(z, x, 1 - core)
    trade_a = pltpu.make_async_remote_copy(
        src_ref=turned_rows.at[1 - core],
        dst_ref=recv_turned,
        send_sem=a_s,
        recv_sem=a_r,
        device_id=sibling,
        device_id_type=MESH,
    )
    trade_a.start()
    trade_b, writes, xcopies, zcopies = [], [], [], []

    def seed_part(q):
        cols = slice(q * wq, (q + 1) * wq)
        msg = jnp.dot(rows[2 + far], wn[:, cols], preferred_element_type=F32).astype(BF16)
        v = s[q] + jnp.dot(adjt[far], msg, preferred_element_type=F32)
        c0 = 0.7978845608028654
        v2 = v * v
        t = jnp.tanh(c0 * v * (1.0 + 0.044715 * v2))
        cdf = 0.5 * (1.0 + t)
        hid[q] = (v * cdf).astype(BF16)
        slope = cdf + 0.5 * v * (1.0 - t * t) * (c0 * (1.0 + (3 * 0.044715) * v2))
        gp = (gout[:, cols].astype(F32) * slope).astype(BF16)
        gm = jnp.dot(adj[...], gp, preferred_element_type=F32).astype(BF16)

        @pl.when(core == 0)
        def _():
            bcat[q, 0:seeds, :] = gp
            bsend[q] = gm

        @pl.when(core != 0)
        def _():
            bcat[q, 0:seeds, :] = gm
            bsend[q] = gp

        copy = pltpu.make_async_remote_copy(
            src_ref=bsend.at[q],
            dst_ref=bcat.at[q, pl.ds(seeds, seeds)],
            send_sem=b_s.at[q],
            recv_sem=b_r.at[q],
            device_id=sibling,
            device_id_type=MESH,
        )
        copy.start()
        trade_b.append(copy)
        write = pltpu.make_async_copy(hid.at[q], hid_hbm.at[:, pl.ds(q * wq, wq)], hsem.at[q])
        write.start()
        writes.append(write)

    peer = dev(z, 1 - x, core)

    def chip_sum(q, half):
        return (
            jnp.dot(turned_rows[core, half], bcat[q, 0:seeds, :], preferred_element_type=F32)
            + jnp.dot(recv_turned[half], bcat[q, seeds : 2 * seeds, :], preferred_element_type=F32)
        ).reshape(NZ, chip_rows, wq)

    def x_part(q):
        trade_b[q].wait_recv()
        xsend[q] = chip_sum(q, 1 - x).astype(BF16)
        for k in (2, 1, 3, 0):
            zb = z_xor(k)
            copy = pltpu.make_async_remote_copy(
                src_ref=xsend.at[q, zb],
                dst_ref=xrecv.at[q, zb],
                send_sem=x_s.at[q, k],
                recv_sem=x_r.at[q, k],
                device_id=peer,
                device_id_type=MESH,
            )
            copy.start()
            xcopies.append(copy)
        gk[q] = chip_sum(q, x)

    def z_part(q):
        for k in (2, 1, 3, 0):
            zb = z_xor(k)
            xcopies[q * NZ + (2, 1, 3, 0).index(k)].wait_recv()
            total = gk[q, zb] + xrecv[q, zb].astype(F32)
            zsend[q, zb] = total.astype(BF16).reshape(NC, chip_rows // NC, wq)
            for i in range(NC):
                cc = 1 - core if i == 0 else core
                if k == 0 and i == 1:
                    zrecv[q, core, z] = zsend[q, z, core]
                    continue
                copy = pltpu.make_async_remote_copy(
                    src_ref=zsend.at[q, zb, cc],
                    dst_ref=zrecv.at[q, core, z],
                    send_sem=z_s.at[q, k, i],
                    recv_sem=z_r.at[q, core, z],
                    device_id=dev(zb, x, cc),
                    device_id_type=MESH,
                )
                copy.start()
                zcopies.append(copy)

    def last_part(q):
        for i in range(NC):
            for k in range(NZ):
                if i == 0 and k == 0:
                    continue
                g = core if i == 0 else 1 - core
                where = zrecv.at[q, g, z_xor(k)]
                pltpu.make_async_remote_copy(
                    src_ref=where,
                    dst_ref=where,
                    send_sem=z_s.at[0, 0, 0],
                    recv_sem=z_r.at[q, g, z_xor(k)],
                    device_id=sibling,
                    device_id_type=MESH,
                ).wait_recv()
        for g, (out, out_hbm) in enumerate(((gs, gs_hbm), (gn, gn_hbm))):
            parts = zrecv[q, g].astype(F32)
            out[q] = (parts[0] + parts[1]) + (parts[2] + parts[3])
            write = pltpu.make_async_copy(
                out.at[q], out_hbm.at[:, pl.ds(q * wq, wq)], osem.at[q, g]
            )
            write.start()
            writes.append(write)

    seed_part(0)
    trade_a.wait_recv()
    x_part(0)
    for q in range(1, nq):
        seed_part(q)
    x_part(1)
    for q in range(nq):
        z_part(q)
        if q + 2 < nq:
            x_part(q + 2)
    for q in range(nq):
        last_part(q)
    for copy in ask + answer + [trade_a] + trade_b + xcopies + zcopies:
        copy.wait_send()
    for write in writes:
        write.wait()


def kernel_body(
    features,
    seed_rows,
    request_rows,
    block_counts,
    tiles,
    tile_seed_block,
    w_self,
    w_neigh,
    grad_out,
):
    n, cap, block = request_rows.shape[1:]
    per = cap * block
    node_count, width = features.shape
    seeds, hidden_width = grad_out.shape
    nq = 4
    wq = hidden_width // nq
    chip_rows = width // (NZ * NX)
    out_rows = width // n
    vmem = pl.BlockSpec(memory_space=pltpu.VMEM)
    smem = pl.BlockSpec(memory_space=pltpu.SMEM)
    hbm = pl.BlockSpec(memory_space=pltpu.HBM)
    dma = pltpu.SemaphoreType.DMA
    results = pl.pallas_call(
        kernel,
        out_shape=(
            jax.ShapeDtypeStruct((seeds, hidden_width), BF16),
            jax.ShapeDtypeStruct((out_rows, hidden_width), F32),
            jax.ShapeDtypeStruct((out_rows, hidden_width), F32),
        ),
        in_specs=[vmem, smem] + [vmem] * 3 + [hbm] * 4,
        out_specs=(hbm,) * 3,
        scratch_shapes=[
            pltpu.VMEM((node_count, width), BF16),
            pltpu.VMEM((width, hidden_width), BF16),
            pltpu.VMEM((width, hidden_width), BF16),
            pltpu.VMEM((seeds, hidden_width), BF16),
            pltpu.VMEM((seeds, node_count), BF16),
            pltpu.VMEM((LANES, LANES), jnp.int32),
            pltpu.VMEM((n, 1, LANES), jnp.int32),
            pltpu.VMEM((n, 1, LANES), jnp.int32),
            pltpu.VMEM((2, n // 2, per, width), BF16),
            pltpu.VMEM((4, LANES, width), BF16),
            pltpu.VMEM((seeds, seeds), F32),
            pltpu.VMEM((seeds, seeds), BF16),
            pltpu.VMEM((2, seeds, LANES), BF16),
            pltpu.VMEM((nq, seeds, wq), F32),
            pltpu.VMEM((nq, seeds, wq), BF16),
            pltpu.VMEM((nq, out_rows, wq), F32),
            pltpu.VMEM((nq, out_rows, wq), F32),
            pltpu.VMEM((2, NX, NZ * chip_rows, seeds), BF16),
            pltpu.VMEM((NX, NZ * chip_rows, seeds), BF16),
            pltpu.VMEM((nq, 2 * seeds, wq), BF16),
            pltpu.VMEM((nq, seeds, wq), BF16),
            pltpu.VMEM((nq, NZ, chip_rows, wq), BF16),
            pltpu.VMEM((nq, NZ, chip_rows, wq), BF16),
            pltpu.VMEM((nq, NZ, chip_rows, wq), F32),
            pltpu.VMEM((nq, NZ, NC, out_rows, wq), BF16),
            pltpu.VMEM((nq, NC, NZ, out_rows, wq), BF16),
            dma((4,)),
            dma((nq + 1,)),
            dma((nq, NC)),
            dma((n - 1,)),
            dma((n,)),
            dma((2, n // 2)),
            dma((n,)),
            dma,
            dma,
            dma((nq,)),
            dma((nq,)),
            dma((nq, NZ)),
            dma((nq, NZ)),
            dma((nq, NZ, NC)),
            dma((nq, NC, NZ)),
        ],
        compiler_params=pltpu.CompilerParams(
            collective_id=0, has_side_effects=True, vmem_limit_bytes=62 * 1024 * 1024
        ),
        name="layer_step",
    )(
        block_counts,
        tile_seed_block,
        jnp.transpose(request_rows[0], (1, 2, 0)),
        seed_rows.reshape(-1, LANES),
        tiles[0],
        features,
        w_self,
        w_neigh,
        grad_out,
    )
    return pl.pallas_call(
        hand_out,
        out_shape=tuple(jax.ShapeDtypeStruct(r.shape, r.dtype) for r in results),
        in_specs=[hbm] * 3,
        out_specs=(hbm,) * 3,
        scratch_shapes=[pltpu.VMEM(r.shape, r.dtype) for r in results] + [dma((2, 4))],
        compiler_params=pltpu.CompilerParams(vmem_limit_bytes=62 * 1024 * 1024),
        name="hand_out",
    )(*results)


def hand_out(a_ref, b_ref, c_ref, a_out, b_out, c_out, a_mid, b_mid, c_mid, sem):
    half = a_ref.shape[0] // 2
    stages = ((b_ref, b_mid, b_out), (c_ref, c_mid, c_out)) + tuple(
        tuple(r.at[pl.ds(i * half, half)] for r in (a_ref, a_mid, a_out)) for i in range(2)
    )
    fetches = [
        pltpu.make_async_copy(src, mid, sem.at[0, i]) for i, (src, mid, _) in enumerate(stages)
    ]
    for fetch in fetches:
        fetch.start()
    stores = []
    for i, (_, mid, out) in enumerate(stages):
        fetches[i].wait()
        stores.append(pltpu.make_async_copy(mid, out, sem.at[1, i]))
        stores[-1].start()
    for store in stores:
        store.wait()


def solution(mesh):
    in_specs = (
        P("shard", None),
        P(("group", "shard")),
        P(("group", "shard"), None, None, None),
        P(("group", "shard"), None),
        P(("group", "shard"), None, None, None),
        P(("group", "shard"), None),
        P(),
        P(),
        P(("group", "shard"), None),
    )
    out_specs = (
        P(("group", "shard"), None),
        P(("group", "shard"), None),
        P(("group", "shard"), None),
    )
    body = kernel_body if mesh.shape["shard"] == NZ * NX * NC else generic_body
    return jax.shard_map(body, mesh=mesh, in_specs=in_specs, out_specs=out_specs, check_vma=False)
```

```python
import functools

import jax
import jax.numpy as jnp
from jax import lax
from jax.experimental import pallas as pl
from jax.experimental.pallas import tpu as pltpu
from jax.sharding import PartitionSpec as P

MESH = pl.DeviceIdType.MESH
BF16 = jnp.bfloat16
F32 = jnp.float32
LANES = 128
NZ, NX, NC = 4, 2, 2
ORDER = (3, 1, 2, 0)


def activate(values):
    return jax.nn.gelu(values, approximate=True)


def generic_body(
    features,
    seed_rows,
    request_rows,
    block_counts,
    tiles,
    tile_seed_block,
    w_self,
    w_neigh,
    grad_out,
):
    requests = request_rows[0]
    slot_count = requests.shape[1]
    feature_width = features.shape[1]
    usable = jnp.arange(slot_count, dtype=jnp.int32)[None, :] < block_counts[0][:, None]
    wanted = lax.all_to_all(
        jnp.where(usable[:, :, None], requests, -1), "shard", split_axis=0, concat_axis=0, tiled=True
    )
    selected_blocks = features[jnp.maximum(wanted, 0)]
    answered = lax.all_to_all(
        jnp.where(wanted[..., None] >= 0, selected_blocks, jnp.zeros((), features.dtype)),
        "shard",
        split_axis=0,
        concat_axis=0,
        tiled=True,
    )
    neighbour_frontier = answered.reshape(-1, feature_width)
    messages = jnp.dot(neighbour_frontier, w_neigh, preferred_element_type=F32).astype(BF16)
    seed_count = seed_rows.shape[0]
    block_rows = tiles.shape[3]
    blocks = seed_count // block_rows
    select_blocks = tile_seed_block[0][:, None] == jnp.arange(blocks, dtype=jnp.int32)[None, :]
    adjacency_matrix = jnp.where(
        select_blocks[:, None, :, None], tiles[0][:, :, None, :], jnp.zeros((), tiles.dtype)
    ).reshape(-1, seed_count)
    neighbour = jnp.dot(adjacency_matrix.T, messages, preferred_element_type=F32)
    own_rows = features[seed_rows]
    summed = jnp.dot(own_rows, w_self, preferred_element_type=F32) + neighbour
    hidden = activate(summed).astype(BF16)
    _, pullback = jax.vjp(activate, summed)
    grad_pre = pullback(grad_out.astype(F32))[0].astype(BF16)
    grad_self = lax.psum_scatter(
        jnp.dot(own_rows.T, grad_pre, preferred_element_type=F32),
        "shard",
        scatter_dimension=0,
        tiled=True,
    )
    grad_msg = jnp.dot(adjacency_matrix, grad_pre, preferred_element_type=F32).astype(BF16)
    grad_neigh = lax.psum_scatter(
        jnp.dot(neighbour_frontier.T, grad_msg, preferred_element_type=F32),
        "shard",
        scatter_dimension=0,
        tiled=True,
    )
    return (hidden, grad_self, grad_neigh)


def down_rows(row):
    return jnp.broadcast_to(row, (LANES, LANES)).T


def put_one_hot(oh, ids, base, count):
    lane = lax.broadcasted_iota(jnp.int32, (LANES, LANES), 1)
    for c in range(count // LANES):
        oh[base : base + LANES, c * LANES : (c + 1) * LANES] = (
            (ids == lane + c * LANES).astype(F32).astype(BF16)
        )


def kernel(
    counts_ref,
    block_ref,
    wanted_ref,
    seeds_ref,
    tiles_ref,
    feat_hbm,
    ws_hbm,
    wn_hbm,
    go_hbm,
    hid_hbm,
    gs_hbm,
    gn_hbm,
    feat,
    ws,
    wn,
    gout,
    oh,
    turn,
    req_ref,
    reqs,
    ans,
    rows,
    adj32,
    adj,
    adjt,
    s,
    hid,
    gs,
    gn,
    turned_rows,
    recv_turned,
    bcat,
    bsend,
    xsend,
    xrecv,
    gk,
    zsend,
    zmid,
    zrecv,
    lsem,
    hsem,
    osem,
    rq_s,
    rq_r,
    fr_s,
    fr_r,
    a_s,
    a_r,
    b_s,
    b_r,
    x_s,
    x_r,
    z_s,
    z_r,
):
    n = NZ * NX * NC
    me = lax.axis_index("shard")
    z, x, core = me // (NX * NC), (me // NC) % NX, me % NC
    half_n = n // 2
    near, far = me // half_n, 1 - me // half_n
    node_count, width = feat.shape
    per = ans.shape[2]
    nq, wq = hid.shape[0], hid.shape[2]
    seeds = hid.shape[1]

    def dev(zz, xx, cc):
        return {"shard": zz * (NX * NC) + xx * NC + cc}

    def z_xor(k):
        return (z, z + 1 - 2 * (z % 2), lax.rem(z + 2, NZ), NZ - 1 - z)[k]

    loads = [
        pltpu.make_async_copy(src, dst, lsem.at[i])
        for i, (src, dst) in enumerate(
            ((feat_hbm, feat), (ws_hbm, ws), (wn_hbm, wn), (go_hbm, gout))
        )
    ]
    for load in loads:
        load.start()
    barrier = pltpu.get_barrier_semaphore()
    others = [lax.rem(me + k, n) for k in range(1, n)]
    for other in others:
        pl.semaphore_signal(barrier, inc=1, device_id={"shard": other}, device_id_type=MESH)
    cap, block = wanted_ref.shape[:2]
    for j in range(cap):
        turn[j * block : (j + 1) * block, 0:n] = jnp.where(
            j < counts_ref[...], wanted_ref[j], -1
        )
    turned = turn[...].T
    for owner in range(n):
        req_ref[owner] = turned[owner : owner + 1, :]
    pl.semaphore_wait(barrier, n - 1)

    chip_rows = width // (NZ * NX)

    def put_turned(kind, h):
        turned = rows[2 * kind + h].T
        lanes = pl.ds(pl.multiple_of(h * LANES, LANES), LANES)
        for zz in range(NZ):
            for xx in range(NX):
                start = (zz * NX + xx) * chip_rows
                turned_rows[kind, xx, zz * chip_rows : (zz + 1) * chip_rows, lanes] = turned[
                    start : start + chip_rows, :
                ]

    ask = []
    for k, owner in enumerate(others):
        ask.append(
            pltpu.make_async_remote_copy(
                src_ref=req_ref.at[owner],
                dst_ref=reqs.at[me],
                send_sem=rq_s.at[k],
                recv_sem=rq_r.at[me],
                device_id={"shard": owner},
                device_id_type=MESH,
            )
        )
        ask[-1].start()
    reqs[me] = req_ref[me]

    answer = []
    for step, h in enumerate((far, near)):
        for j in range(half_n):
            src = h * half_n + j

            @pl.when(src != me)
            def _():
                pltpu.make_async_remote_copy(
                    src_ref=reqs.at[src],
                    dst_ref=reqs.at[src],
                    send_sem=rq_s.at[0],
                    recv_sem=rq_r.at[src],
                    device_id={"shard": others[0]},
                    device_id_type=MESH,
                ).wait_recv()
            turn[j : j + 1, :] = reqs[src]
        turned = turn[...].T
        wanted = [
            jnp.broadcast_to(turned[0:per, j : j + 1], (per, LANES)) for j in range(half_n)
        ]
        put_one_hot(oh, jnp.concatenate(wanted, axis=0), 0, node_count)
        if step == 0:
            loads[0].wait()
        ans[h] = (
            jnp.dot(oh[0:LANES, :], feat[...], preferred_element_type=F32)
            .astype(BF16)
            .reshape(half_n, per, width)
        )
        mine = rows.at[2 + near, pl.ds(pl.multiple_of((me % half_n) * per, per), per)]
        for j in range(half_n):
            slot = lax.rem(me + j, half_n)
            dst = h * half_n + slot
            if step == 1 and j == 0:
                own = pltpu.make_async_copy(ans.at[h, slot], mine, hsem.at[nq])
                own.start()
                continue
            copy = pltpu.make_async_remote_copy(
                src_ref=ans.at[h, slot],
                dst_ref=mine,
                send_sem=fr_s.at[step, j],
                recv_sem=fr_r.at[me],
                device_id={"shard": dst},
                device_id_type=MESH,
            )
            copy.start()
            answer.append(copy)

    for h in range(seeds // LANES):
        put_one_hot(oh, down_rows(seeds_ref[h : h + 1, :]), h * LANES, node_count)
    for h in range(seeds // LANES):
        rows[h] = jnp.dot(
            oh[h * LANES : (h + 1) * LANES, :], feat[...], preferred_element_type=F32
        ).astype(BF16)

    for slot in range(tiles_ref.shape[0]):
        tile = tiles_ref[slot].astype(F32)
        for b in range(seeds // LANES):
            adj32[slot * block : (slot + 1) * block, b * LANES : (b + 1) * LANES] = jnp.where(
                block_ref[0, slot] == b, tile, 0.0
            )
    adj[...] = adj32[...].astype(BF16)
    for h in range(2):
        adjt[h] = adj32[h * LANES : (h + 1) * LANES, :].T.astype(BF16)
    loads[1].wait()
    own_rows = rows[0:2].reshape(seeds, width)
    for q in range(nq):
        s[q] = jnp.dot(own_rows, ws[:, q * wq : (q + 1) * wq], preferred_element_type=F32)
    loads[2].wait()
    loads[3].wait()

    def wait_rows(h, skip_me):
        for j in range(half_n):
            owner = h * half_n + j

            def wait():
                where = rows.at[2 + h, pl.ds(j * per, per)]
                pltpu.make_async_remote_copy(
                    src_ref=where,
                    dst_ref=where,
                    send_sem=fr_s.at[0, 0],
                    recv_sem=fr_r.at[owner],
                    device_id={"shard": others[0]},
                    device_id_type=MESH,
                ).wait_recv()

            if skip_me:
                pl.when(owner != me)(wait)
            else:
                wait()

    put_turned(0, 0)
    put_turned(0, 1)
    own.wait()
    wait_rows(near, True)
    put_turned(1, near)
    for q in range(nq):
        msg = jnp.dot(
            rows[2 + near], wn[:, q * wq : (q + 1) * wq], preferred_element_type=F32
        ).astype(BF16)
        s[q] += jnp.dot(adjt[near], msg, preferred_element_type=F32)
    wait_rows(far, False)
    put_turned(1, far)

    sibling = dev(z, x, 1 - core)
    trade_a = pltpu.make_async_remote_copy(
        src_ref=turned_rows.at[1 - core],
        dst_ref=recv_turned,
        send_sem=a_s,
        recv_sem=a_r,
        device_id=sibling,
        device_id_type=MESH,
    )
    trade_a.start()
    trade_b, writes, xcopies, zcopies = [], [], [], []

    def seed_part(q):
        cols = slice(q * wq, (q + 1) * wq)
        msg = jnp.dot(rows[2 + far], wn[:, cols], preferred_element_type=F32).astype(BF16)
        v = s[q] + jnp.dot(adjt[far], msg, preferred_element_type=F32)
        c0 = 0.7978845608028654
        v2 = v * v
        t = jnp.tanh(c0 * v * (1.0 + 0.044715 * v2))
        cdf = 0.5 * (1.0 + t)
        hid[q] = (v * cdf).astype(BF16)
        slope = cdf + 0.5 * v * (1.0 - t * t) * (c0 * (1.0 + (3 * 0.044715) * v2))
        gp = (gout[:, cols].astype(F32) * slope).astype(BF16)
        gm = jnp.dot(adj[...], gp, preferred_element_type=F32).astype(BF16)

        @pl.when(core == 0)
        def _():
            bcat[q, 0:seeds, :] = gp
            bsend[q] = gm

        @pl.when(core != 0)
        def _():
            bcat[q, 0:seeds, :] = gm
            bsend[q] = gp

        copy = pltpu.make_async_remote_copy(
            src_ref=bsend.at[q],
            dst_ref=bcat.at[q, pl.ds(seeds, seeds)],
            send_sem=b_s.at[q],
            recv_sem=b_r.at[q],
            device_id=sibling,
            device_id_type=MESH,
        )
        copy.start()
        trade_b.append(copy)
        write = pltpu.make_async_copy(hid.at[q], hid_hbm.at[:, pl.ds(q * wq, wq)], hsem.at[q])
        write.start()
        writes.append(write)

    peer = dev(z, 1 - x, core)

    def chip_sum(q, half):
        return (
            jnp.dot(turned_rows[core, half], bcat[q, 0:seeds, :], preferred_element_type=F32)
            + jnp.dot(recv_turned[half], bcat[q, seeds : 2 * seeds, :], preferred_element_type=F32)
        ).reshape(NZ, chip_rows, wq)

    def x_part(q):
        trade_b[q].wait_recv()
        xsend[q] = chip_sum(q, 1 - x).astype(BF16)
        for k in ORDER:
            zb = z_xor(k)
            copy = pltpu.make_async_remote_copy(
                src_ref=xsend.at[q, zb],
                dst_ref=xrecv.at[q, zb],
                send_sem=x_s.at[q, k],
                recv_sem=x_r.at[q, k],
                device_id=peer,
                device_id_type=MESH,
            )
            copy.start()
            xcopies.append(copy)
        gk[q] = chip_sum(q, x)

    def piece(q, k):
        zb = z_xor(k)
        xcopies[q * NZ + ORDER.index(k)].wait_recv()
        return (gk[q, zb] + xrecv[q, zb].astype(F32)).reshape(NC, chip_rows // NC, wq)

    def z_send(src, dst, send_sem, recv_sem, device):
        copy = pltpu.make_async_remote_copy(
            src_ref=src,
            dst_ref=dst,
            send_sem=send_sem,
            recv_sem=recv_sem,
            device_id=device,
            device_id_type=MESH,
        )
        copy.start()
        zcopies.append(copy)
        return copy

    pairs = []

    def z_pair(q):
        for i, k in ((1, 3), (0, 1)):
            zb = z_xor(k)
            zsend[q, zb] = piece(q, k).astype(BF16)
            pairs.append(
                z_send(
                    zsend.at[q, zb],
                    zmid.at[q, i],
                    z_s.at[q, 0, i],
                    z_r.at[q, i, 2],
                    dev(z_xor(1), x, core),
                )
            )

    def z_cross(q):
        across = z_xor(2)
        total = piece(q, 2)
        pairs[2 * q].wait_recv()
        zsend[q, across] = (total + zmid[q, 1].astype(F32)).astype(BF16)
        for cc in range(NC):
            z_send(
                zsend.at[q, across, cc],
                zrecv.at[q, core, 0],
                z_s.at[q, 1, cc],
                z_r.at[q, core, 0],
                dev(across, x, cc),
            )
        total = piece(q, 0)
        pairs[2 * q + 1].wait_recv()
        zsend[q, z] = (total + zmid[q, 0].astype(F32)).astype(BF16)
        z_send(
            zsend.at[q, z, 1 - core],
            zrecv.at[q, core, 1],
            z_s.at[q, 2, 0],
            z_r.at[q, core, 1],
            sibling,
        )
        zrecv[q, core, 1] = zsend[q, z, core]

    def last_part(q):
        for g, i in ((1 - core, 1), (0, 0), (1, 0)):
            where = zrecv.at[q, g, i]
            pltpu.make_async_remote_copy(
                src_ref=where,
                dst_ref=where,
                send_sem=z_s.at[0, 0, 0],
                recv_sem=z_r.at[q, g, i],
                device_id=sibling,
                device_id_type=MESH,
            ).wait_recv()
        for g, (out, out_hbm) in enumerate(((gs, gs_hbm), (gn, gn_hbm))):
            parts = zrecv[q, g].astype(F32)
            out[q] = parts[0] + parts[1]
            write = pltpu.make_async_copy(
                out.at[q], out_hbm.at[:, pl.ds(q * wq, wq)], osem.at[q, g]
            )
            write.start()
            writes.append(write)

    seed_part(0)
    trade_a.wait_recv()
    x_part(0)
    for q in range(1, nq):
        seed_part(q)
    x_part(1)
    for q in range(nq):
        z_pair(q)
        if q + 2 < nq:
            x_part(q + 2)
        z_cross(q)
    for q in range(nq):
        last_part(q)
    for copy in ask + answer + [trade_a] + trade_b + xcopies + zcopies:
        copy.wait_send()
    for write in writes:
        write.wait()


def kernel_body(
    features,
    seed_rows,
    request_rows,
    block_counts,
    tiles,
    tile_seed_block,
    w_self,
    w_neigh,
    grad_out,
):
    n, cap, block = request_rows.shape[1:]
    per = cap * block
    node_count, width = features.shape
    seeds, hidden_width = grad_out.shape
    nq = 4
    wq = hidden_width // nq
    chip_rows = width // (NZ * NX)
    out_rows = width // n
    vmem = pl.BlockSpec(memory_space=pltpu.VMEM)
    smem = pl.BlockSpec(memory_space=pltpu.SMEM)
    hbm = pl.BlockSpec(memory_space=pltpu.HBM)
    dma = pltpu.SemaphoreType.DMA
    results = pl.pallas_call(
        kernel,
        out_shape=(
            jax.ShapeDtypeStruct((seeds, hidden_width), BF16),
            jax.ShapeDtypeStruct((out_rows, hidden_width), F32),
            jax.ShapeDtypeStruct((out_rows, hidden_width), F32),
        ),
        in_specs=[vmem, smem] + [vmem] * 3 + [hbm] * 4,
        out_specs=(hbm,) * 3,
        scratch_shapes=[
            pltpu.VMEM((node_count, width), BF16),
            pltpu.VMEM((width, hidden_width), BF16),
            pltpu.VMEM((width, hidden_width), BF16),
            pltpu.VMEM((seeds, hidden_width), BF16),
            pltpu.VMEM((seeds, node_count), BF16),
            pltpu.VMEM((LANES, LANES), jnp.int32),
            pltpu.VMEM((n, 1, LANES), jnp.int32),
            pltpu.VMEM((n, 1, LANES), jnp.int32),
            pltpu.VMEM((2, n // 2, per, width), BF16),
            pltpu.VMEM((4, LANES, width), BF16),
            pltpu.VMEM((seeds, seeds), F32),
            pltpu.VMEM((seeds, seeds), BF16),
            pltpu.VMEM((2, seeds, LANES), BF16),
            pltpu.VMEM((nq, seeds, wq), F32),
            pltpu.VMEM((nq, seeds, wq), BF16),
            pltpu.VMEM((nq, out_rows, wq), F32),
            pltpu.VMEM((nq, out_rows, wq), F32),
            pltpu.VMEM((2, NX, NZ * chip_rows, seeds), BF16),
            pltpu.VMEM((NX, NZ * chip_rows, seeds), BF16),
            pltpu.VMEM((nq, 2 * seeds, wq), BF16),
            pltpu.VMEM((nq, seeds, wq), BF16),
            pltpu.VMEM((nq, NZ, chip_rows, wq), BF16),
            pltpu.VMEM((nq, NZ, chip_rows, wq), BF16),
            pltpu.VMEM((nq, NZ, chip_rows, wq), F32),
            pltpu.VMEM((nq, NZ, NC, out_rows, wq), BF16),
            pltpu.VMEM((nq, 2, NC, out_rows, wq), BF16),
            pltpu.VMEM((nq, NC, 2, out_rows, wq), BF16),
            dma((4,)),
            dma((nq + 1,)),
            dma((nq, NC)),
            dma((n - 1,)),
            dma((n,)),
            dma((2, n // 2)),
            dma((n,)),
            dma,
            dma,
            dma((nq,)),
            dma((nq,)),
            dma((nq, NZ)),
            dma((nq, NZ)),
            dma((nq, NZ, NC)),
            dma((nq, NC, 3)),
        ],
        compiler_params=pltpu.CompilerParams(
            collective_id=0, has_side_effects=True, vmem_limit_bytes=62 * 1024 * 1024
        ),
        name="layer_step",
    )(
        block_counts,
        tile_seed_block,
        jnp.transpose(request_rows[0], (1, 2, 0)),
        seed_rows.reshape(-1, LANES),
        tiles[0],
        features,
        w_self,
        w_neigh,
        grad_out,
    )
    return pl.pallas_call(
        hand_out,
        out_shape=tuple(jax.ShapeDtypeStruct(r.shape, r.dtype) for r in results),
        in_specs=[hbm] * 3,
        out_specs=(hbm,) * 3,
        scratch_shapes=[pltpu.VMEM(r.shape, r.dtype) for r in results] + [dma((2, 4))],
        compiler_params=pltpu.CompilerParams(vmem_limit_bytes=62 * 1024 * 1024),
        name="hand_out",
    )(*results)


def hand_out(a_ref, b_ref, c_ref, a_out, b_out, c_out, a_mid, b_mid, c_mid, sem):
    half = a_ref.shape[0] // 2
    stages = ((b_ref, b_mid, b_out), (c_ref, c_mid, c_out)) + tuple(
        tuple(r.at[pl.ds(i * half, half)] for r in (a_ref, a_mid, a_out)) for i in range(2)
    )
    fetches = [
        pltpu.make_async_copy(src, mid, sem.at[0, i]) for i, (src, mid, _) in enumerate(stages)
    ]
    for fetch in fetches:
        fetch.start()
    stores = []
    for i, (_, mid, out) in enumerate(stages):
        fetches[i].wait()
        stores.append(pltpu.make_async_copy(mid, out, sem.at[1, i]))
        stores[-1].start()
    for store in stores:
        store.wait()


def solution(mesh):
    in_specs = (
        P("shard", None),
        P(("group", "shard")),
        P(("group", "shard"), None, None, None),
        P(("group", "shard"), None),
        P(("group", "shard"), None, None, None),
        P(("group", "shard"), None),
        P(),
        P(),
        P(("group", "shard"), None),
    )
    out_specs = (
        P(("group", "shard"), None),
        P(("group", "shard"), None),
        P(("group", "shard"), None),
    )
    body = kernel_body if mesh.shape["shard"] == NZ * NX * NC else generic_body
    return jax.shard_map(body, mesh=mesh, in_specs=in_specs, out_specs=out_specs, check_vma=False)
```
